512 devices in a mesh: row: 16 (over z, core), col: 32 (over x, y).
Axes of the slice: x: 4, y: 8, z: 8, core: 2. Of those that a mesh axis runs over, the one named last changes fastest.
Arguments:
- slip_load: bfloat16 [16, 32, 1024, 128], P('row', 'col'), may hold values from -6 to 6
- flexibility: bfloat16 [16, 32, 1024, 1024], P('row', 'col'), as said below
- schur: bfloat16 [16, 32, 1024, 1024], P('row', 'col'), as said below
- corner_coupling: float32 [16, 32, 12, 1024], P('row', 'col'), may hold values from -0.1875 to 0.1875
- coarse_inverse: float32 [6144, 6144], P('row', 'col'), as said below
- bounds_table: float32 [16], replicated, may hold values from 0.3 to 3
- bound_index: int32 [16, 32, 1024], P('row', 'col'), may hold values from 0 to 15
- face_rows: int32 [16, 32, 4], P('row', 'col'), may hold values from 0 to 256, as said below
Outputs:
- multipliers: bfloat16 [16, 32, 1024, 128], P('row', 'col')
The draws below stay inside these ranges and needn't reach their ends.
Inputs may be any that keep to these rules, and one draw needn't show every extreme that they name: `face_rows`: face counts agree between the two subdomains of a shared face, are 0 on faces at the edge of the grid, and some face has exactly 256 live slots. `coarse_inverse`: symmetric. `flexibility`: symmetric and positive definite. `schur`: symmetric and positive definite.
All inputs are finite; a program needn't handle non-finite values.
Results may differ from the reference program's by a relative error of at most 0.0038.
Values sent between devices are 32-bit elements; how exact they have to be, the bound alone decides.
A program may use at most 64 MiB of HBM per device.

```python
import math
import jax
import jax.numpy as jnp
from jax import lax

M = 1024
NC = 12
R = 128
LEVELS = 16
ITERS = 2
FACE = 256
NCO = 6144
N_ROW = 16
N_COL = 32


def dominant_blocks(key, spread_low, spread_high):

    def one_block(index):
        block_key = jax.random.fold_in(key, index)
        first_key, second_key, third_key = jax.random.split(block_key, 3)
        raw = jax.random.normal(first_key, (M, M), jnp.float32)
        symmetric = (raw + raw.T) / jnp.sqrt(2.0 * M)
        diagonal = jax.random.uniform(second_key, (M,), jnp.float32, spread_low, spread_high)
        material = jnp.exp(jax.random.uniform(third_key, (), jnp.float32, -1.5, 1.5))
        return ((symmetric + jnp.diag(diagonal)) * material).astype(jnp.bfloat16)
    blocks = lax.map(one_block, jnp.arange(N_ROW * N_COL, dtype=jnp.int32))
    return blocks.reshape(N_ROW, N_COL, M, M)


def draw_flexibility(key, part):
    inner = jax.random.fold_in(key, 11)
    return dominant_blocks(inner, 2.5, 4.0)


def draw_schur(key, part):
    inner = jax.random.fold_in(key, 23)
    return dominant_blocks(inner, 2.5, 4.0)


def draw_coarse_inverse(key, part):
    inner = jax.random.fold_in(key, 37)
    first_key, second_key = jax.random.split(inner)
    raw = jax.random.normal(first_key, (NCO, NCO), jnp.float32)
    symmetric = (raw + raw.T) / jnp.sqrt(2.0 * NCO)
    diagonal = jax.random.uniform(second_key, (NCO,), jnp.float32, 4.0, 8.0)
    return symmetric + jnp.diag(diagonal)


def draw_face_rows(key, part):
    inner = jax.random.fold_in(key, 41)
    first_key, second_key = jax.random.split(inner)
    horizontal = jax.random.randint(first_key, (N_ROW, N_COL - 1), FACE // 8, FACE + 1, jnp.int32)
    horizontal = horizontal.at[0, 0].set(FACE)
    vertical = jax.random.randint(second_key, (N_ROW - 1, N_COL), FACE // 8, FACE + 1, jnp.int32)
    west_side = jnp.pad(horizontal, ((0, 0), (1, 0)))
    east_side = jnp.pad(horizontal, ((0, 0), (0, 1)))
    lower_side = jnp.pad(vertical, ((1, 0), (0, 0)))
    upper_side = jnp.pad(vertical, ((0, 1), (0, 0)))
    return jnp.stack([west_side, east_side, lower_side, upper_side], axis=-1)


def plant(values, own_key, least, high):
    place = [jax.random.randint(jax.random.fold_in(own_key, axis), (), 0, length) for axis, length in enumerate(values.shape)]
    widest = values.shape.index(max(values.shape))
    neighbour = place[:widest] + [(place[widest] + 1) % values.shape[widest]] + place[widest + 1:]
    return values.at[tuple(place)].set(least).at[tuple(neighbour)].set(high)


def steps_of(key, extent, shards, low, high):
    level = 1.0
    for dim, parts in shards:
        steps = jax.random.uniform(jax.random.fold_in(jax.random.fold_in(key, 6), dim), (parts,), jnp.float32, low / len(shards), high / len(shards))
        level = level * jnp.repeat(jnp.exp(steps), extent[dim] // parts).reshape((-1,) + (1,) * (len(extent) - 1 - dim))
    return level


def bell_draw(rng, extent, scale, most, pieces=(), kind=jnp.bfloat16):
    entries = jax.random.normal(rng, extent, jnp.float32) * scale
    if len(pieces) > 0:
        entries = steps_of(rng, extent, pieces, -0.22, 0.18) * entries
    return jnp.clip(entries, min=-most, max=most).astype(kind)


def setup_inputs(seed: int = 0) -> dict:
    key_of = jax.random.split(jax.random.key(seed), 9)
    slip_load = bell_draw(key_of[0], (N_ROW, N_COL, M, R), 1.0, 6.0, ((0, 16), (1, 32)))
    flexibility = draw_flexibility(jax.random.fold_in(key_of[8], 71), 0)
    schur = draw_schur(jax.random.fold_in(key_of[8], 71), 0)
    corner_coupling = bell_draw(key_of[3], (N_ROW, N_COL, NC, M), M ** -0.5, 0.1875, ((0, 16), (1, 32)), jnp.float32)
    coarse_inverse = draw_coarse_inverse(jax.random.fold_in(key_of[8], 71), 0)
    bounds_table = jnp.clip(jnp.exp(jax.random.uniform(key_of[5], (LEVELS,), jnp.float32, math.log(0.3), math.log(3.0))), 0.3, 3.0)
    bound_index = plant(jax.random.randint(key_of[6], (N_ROW, N_COL, M), 0, LEVELS), jax.random.fold_in(key_of[6], 1), 0, LEVELS - 1).astype(jnp.int32)
    face_rows = draw_face_rows(jax.random.fold_in(key_of[8], 71), 0)
    return dict(slip_load=slip_load, flexibility=flexibility, schur=schur, corner_coupling=corner_coupling, coarse_inverse=coarse_inverse, bounds_table=bounds_table, bound_index=bound_index, face_rows=face_rows)


def blockwise(matrices, vectors):
    def product(operands):
        return jnp.dot(operands[0], operands[1], preferred_element_type=jnp.float32)
    return lax.map(product, (matrices, vectors))


def reference(slip_load, flexibility, schur, corner_coupling, coarse_inverse, bounds_table, bound_index, face_rows):
    count = N_ROW * N_COL
    flex_flat = flexibility.reshape(count, M, M)
    schur_flat = schur.reshape(count, M, M)
    levels = jnp.arange(LEVELS, dtype=jnp.int32)
    onehot = (bound_index[..., None] == levels).astype(jnp.float32)
    bound = jnp.sum(onehot * bounds_table.astype(jnp.float32), axis=-1)[..., None]
    slots = jnp.arange(FACE, dtype=jnp.int32)
    live = (slots[None, None, None, :] < face_rows[..., None]).astype(jnp.float32).reshape(N_ROW, N_COL, M, 1)
    loads = slip_load.astype(jnp.float32)
    lam = jnp.clip(loads, -bound, bound)
    for iteration in range(ITERS):
        displacement = blockwise(flex_flat, lam.astype(jnp.bfloat16).reshape(count, M, R)).reshape(N_ROW, N_COL, M, R)
        west_face = displacement[:, :, 0:FACE]
        east_face = displacement[:, :, FACE:2 * FACE]
        lower_face = displacement[:, :, 2 * FACE:3 * FACE]
        upper_face = displacement[:, :, 3 * FACE:]
        nb_west = jnp.pad(east_face[:, :-1], ((0, 0), (1, 0), (0, 0), (0, 0)))
        nb_east = jnp.pad(west_face[:, 1:], ((0, 0), (0, 1), (0, 0), (0, 0)))
        nb_lower = jnp.pad(upper_face[:-1], ((1, 0), (0, 0), (0, 0), (0, 0)))
        nb_upper = jnp.pad(lower_face[1:], ((0, 1), (0, 0), (0, 0), (0, 0)))
        paired = jnp.concatenate([nb_west, nb_east, nb_lower, nb_upper], axis=2)
        jump = live * (displacement - paired - loads)
        corner_force = jnp.einsum('rcki,rcin->rckn', corner_coupling.astype(jnp.float32), jump, precision=lax.Precision.HIGHEST)
        ordered = jnp.transpose(corner_force, (1, 0, 2, 3)).reshape(N_COL * N_ROW * NC, R)
        solved = jnp.dot(coarse_inverse.astype(jnp.float32), ordered, precision=lax.Precision.HIGHEST)
        coarse = jnp.transpose(solved.reshape(N_COL, N_ROW, NC, R), (1, 0, 2, 3))
        projected = jump - jnp.einsum('rcki,rckn->rcin', corner_coupling.astype(jnp.float32), coarse, precision=lax.Precision.HIGHEST)
        projected_b = projected.astype(jnp.bfloat16)
        search = blockwise(schur_flat, projected_b.reshape(count, M, R)).reshape(N_ROW, N_COL, M, R)
        search_b = search.astype(jnp.bfloat16)
        curved = blockwise(flex_flat, search_b.reshape(count, M, R)).reshape(N_ROW, N_COL, M, R)
        gain = jnp.sum(projected_b.astype(jnp.float32) * search, axis=(0, 1, 2))
        curvature = jnp.sum(search_b.astype(jnp.float32) * curved, axis=(0, 1, 2))
        lam = jnp.clip(lam - (gain / curvature)[None, None, None, :] * search, -bound, bound)
    return lam.astype(jnp.bfloat16)
```

```python
import jax
import jax.numpy as jnp
from jax import lax
from jax.experimental import pallas as pl
from jax.experimental.pallas import tpu as pltpu
from jax.sharding import PartitionSpec as P

MESH = pl.DeviceIdType.MESH
F32 = jnp.float32
BF16 = jnp.bfloat16
ITERS = 2
NR = 16
NCOL = 32
M = 1024
FACE = 256
NC = 12
R = 128
LEVELS = 16


def dot(a, b):
    return jnp.dot(a, b, preferred_element_type=F32)


def split(v):
    high = v.astype(BF16)
    low = (v - high.astype(F32)).astype(BF16)
    return high, low


def kernel(
    slip_h, flex_h, schur_h, coup_h, coarse_h, table, bidx_h, frows, out_ref,
    slip, flex, schur, coup, coarse, bidx,
    bound, lam, disp, paired, jump, search, pb_v, ct, c2,
    asend, arecv, aleft, aright, ahi, alo,
    xsend, xall, part, parts, zsend, zall, psend, pall,
    load_sem, a_sem, face_s, face_r, x_sem, part_sem, z_sem, p_sem,
):
    r = lax.axis_index("row")
    c = lax.axis_index("col")

    loads = [
        pltpu.make_async_copy(coarse_h, coarse, load_sem.at[0]),
        pltpu.make_async_copy(bidx_h.at[0], bidx, load_sem.at[1]),
        pltpu.make_async_copy(slip_h.at[0, 0], slip, load_sem.at[2]),
        pltpu.make_async_copy(flex_h.at[0, 0], flex, load_sem.at[3]),
        pltpu.make_async_copy(coup_h.at[0, 0], coup, load_sem.at[4]),
        pltpu.make_async_copy(schur_h.at[0, 0], schur, load_sem.at[5]),
    ]
    for copy in loads:
        copy.start()

    xall[:, :, NC:16, :] = jnp.zeros((ITERS, NR, 16 - NC, R), F32)

    barrier = pltpu.get_barrier_semaphore()

    def greet_row(k, carry):
        pl.semaphore_signal(barrier, inc=1, device_id=(lax.rem(r + k, NR), c), device_id_type=MESH)
        return carry

    def greet_col(k, carry):
        pl.semaphore_signal(barrier, inc=1, device_id=(r, lax.rem(c + k, NCOL)), device_id_type=MESH)
        return carry

    lax.fori_loop(1, NCOL, greet_col, 0)
    lax.fori_loop(1, NR, greet_row, 0)

    loads[0].wait()
    for a in range(NR):
        lo, hi = a * NC, NR * NC + a * NC
        asend[a, 0:NC, :] = coarse[lo : lo + NC, 0:128]
        asend[a, NC : 2 * NC, :] = coarse[hi : hi + NC, 0:128]
        asend[a, 2 * NC : 3 * NC, 0:64] = coarse[lo : lo + NC, 128:192]
        asend[a, 2 * NC : 3 * NC, 64:128] = coarse[hi : hi + NC, 128:192]

    loads[1].wait()
    for q in range(M // 128):
        level = bidx[:, q * 128 : (q + 1) * 128]
        row = jnp.zeros((1, 128), F32)
        for n in range(LEVELS):
            row = jnp.where(level == n, table[n], row)
        bound[q * 128 : (q + 1) * 128, :] = jnp.transpose(jnp.broadcast_to(row, (128, 128)))

    loads[2].wait()
    lam[...] = jnp.clip(slip[...].astype(F32), -bound[...], bound[...])
    loads[3].wait()

    pl.semaphore_wait(barrier, NR + NCOL - 2)

    def send_a(k, carry):
        to = lax.rem(r + k, NR)
        pltpu.make_async_remote_copy(
            asend.at[to], arecv.at[r], a_sem.at[0], a_sem.at[1], device_id=(to, c), device_id_type=MESH
        ).start()
        return carry

    lax.fori_loop(1, NR, send_a, 0)
    arecv[r] = asend[r]

    loads[4].wait()
    coup_hi, coup_lo = split(coup[...])
    c2[0:NC, :] = coup_hi.astype(F32)
    c2[NC:16, :] = jnp.zeros((4, M), F32)
    c2[16 : 16 + NC, :] = coup_lo.astype(F32)
    c2[16 + NC : 32, :] = jnp.zeros((4, M), F32)
    stacked = jnp.concatenate([c2[...], c2[0:16, :], jnp.zeros((80, M), F32)], axis=0)
    for q in range(M // 128):
        ct[q * 128 : (q + 1) * 128, :] = jnp.transpose(stacked[:, q * 128 : (q + 1) * 128]).astype(BF16)
    loads[5].wait()

    up_col, down_col = lax.rem(c + 1, NCOL), lax.rem(c + NCOL - 1, NCOL)
    up_row, down_row = lax.rem(r + 1, NR), lax.rem(r + NR - 1, NR)
    faces = (
        (1, (r, up_col), 0),
        (0, (r, down_col), 1),
        (3, (up_row, c), 2),
        (2, (down_row, c), 3),
    )

    def unpack_a():
        pltpu.make_async_copy(arecv.at[pl.ds(0, NR - 1)], arecv.at[pl.ds(0, NR - 1)], a_sem.at[1]).wait()
        lane = lax.broadcasted_iota(jnp.int32, (NC, 128), 1)
        zero = jnp.zeros((NC, 128), F32)
        for s in range(NR):
            last = arecv[s, 2 * NC : 3 * NC, :]
            aleft[2 * s, 0:NC, :] = arecv[s, 0:NC, :]
            aleft[2 * s + 1, 0:NC, :] = arecv[s, NC : 2 * NC, :]
            aright[2 * s, 0:NC, :] = jnp.where(lane < 64, last, zero)
            aright[2 * s + 1, 0:NC, :] = jnp.where(lane < 64, zero, last)
        i0 = lax.broadcasted_iota(jnp.int32, (128, 256), 0)
        i1 = lax.broadcasted_iota(jnp.int32, (128, 256), 1)
        index = jnp.where(i1 % 16 < NC, (i1 // 16) * NC + i1 % 16, -1)
        pick_left = (index == i0).astype(F32).astype(BF16)
        pick_right = (index == 128 + i0 % 64).astype(F32).astype(BF16)
        left_hi, left_lo = split(aleft[...].reshape(512, 128))
        right_hi, right_lo = split(aright[...].reshape(512, 128))
        ahi[...] = (dot(left_hi, pick_left) + dot(right_hi, pick_right)).astype(BF16)
        alo[...] = (dot(left_lo, pick_left) + dot(right_lo, pick_right)).astype(BF16)

    aleft[...] = jnp.zeros_like(aleft)
    aright[...] = jnp.zeros_like(aright)

    for it in range(ITERS):
        lam_b = lam[...].astype(BF16)
        for own, to, there in faces:
            rows = slice(own * FACE, (own + 1) * FACE)
            disp[it, rows, :] = dot(flex[rows, :], lam_b)
            pltpu.make_async_remote_copy(
                disp.at[it, pl.ds(own * FACE, FACE)],
                paired.at[it, pl.ds(there * FACE, FACE)],
                face_s.at[it, own],
                face_r.at[it, there],
                device_id=to,
                device_id_type=MESH,
            ).start()
        for f in range(4):
            rows = slice(f * FACE, (f + 1) * FACE)
            landed = paired.at[it, pl.ds(f * FACE, FACE)]
            pltpu.make_async_copy(landed, landed, face_r.at[it, f]).wait()
            live = lax.broadcasted_iota(jnp.int32, (FACE, R), 0) < frows[0, 0, f]
            gap = disp[it, rows, :] - paired[it, rows, :] - slip[rows, :].astype(F32)
            jump[rows, :] = jnp.where(live, gap, 0.0)
        jump_hi, jump_lo = split(jump[...])
        force = dot(c2[...].astype(BF16), jnp.concatenate([jump_hi, jump_lo], axis=1))
        force = force[0:16, 0:R] + (force[0:16, R : 2 * R] + force[16:32, 0:R])
        xsend[it] = force[0:NC, :]
        xall[it, r, 0:NC, :] = force[0:NC, :]

        def send_x(k, carry):
            to = lax.rem(r + k, NR)
            pltpu.make_async_remote_copy(
                xsend.at[it], xall.at[it, r, pl.ds(0, NC)], x_sem.at[it, 0], x_sem.at[it, 1],
                device_id=(to, c), device_id_type=MESH,
            ).start()
            return carry

        lax.fori_loop(1, NR, send_x, 0)
        if it == 0:
            unpack_a()
        landed = xall.at[it, pl.ds(0, NR - 1), pl.ds(0, NC)]
        pltpu.make_async_copy(landed, landed, x_sem.at[it, 1]).wait()
        x_hi, x_lo = split(xall[it].reshape(256, R))
        both = dot(ahi[...], jnp.concatenate([x_hi, x_lo], axis=1))
        sums = both[:, 0:R] + (both[:, R : 2 * R] + dot(alo[...], x_hi))
        part[it] = sums.reshape(NCOL, 16, R)[:, 0:NC, :]
        parts[it, c] = part[it, c]

        def send_part(k, carry):
            to = lax.rem(c + k, NCOL)
            pltpu.make_async_remote_copy(
                part.at[it, to], parts.at[it, c], part_sem.at[it, 0], part_sem.at[it, 1],
                device_id=(r, to), device_id_type=MESH,
            ).start()
            return carry

        lax.fori_loop(1, NCOL, send_part, 0)
        landed = parts.at[it, pl.ds(0, NCOL - 1)]
        pltpu.make_async_copy(landed, landed, part_sem.at[it, 1]).wait()
        values = jnp.sum(parts[it], axis=0)
        values = jnp.concatenate([values, jnp.zeros((4, R), F32)], axis=0)
        v_hi, v_lo = split(values)
        v_hi, v_lo = v_hi.astype(F32), v_lo.astype(F32)
        stack = jnp.concatenate([v_hi, v_hi, v_lo, jnp.zeros((80, R), F32)], axis=0).astype(BF16)
        p_b = (jump[...] - dot(ct[...], stack)).astype(BF16)
        gain = jnp.zeros((1, R), F32)
        pb_v[...] = p_b
        for f in range(4):
            rows = slice(f * FACE, (f + 1) * FACE)
            s = dot(schur[rows, :], p_b)
            search[rows, :] = s
            gain = gain + jnp.sum(pb_v[rows, :].astype(F32) * s, axis=0, keepdims=True)
        s_b = search[...].astype(BF16)
        curve = jnp.zeros((1, R), F32)
        for f in range(4):
            rows = slice(f * FACE, (f + 1) * FACE)
            curve = curve + jnp.sum(
                search[rows, :].astype(BF16).astype(F32) * dot(flex[rows, :], s_b), axis=0, keepdims=True
            )
        both = jnp.concatenate([gain, curve], axis=0)
        zsend[it] = both
        zall[it, r] = both

        def send_z(k, carry):
            to = lax.rem(r + k, NR)
            pltpu.make_async_remote_copy(
                zsend.at[it], zall.at[it, r], z_sem.at[it, 0], z_sem.at[it, 1],
                device_id=(to, c), device_id_type=MESH,
            ).start()
            return carry

        lax.fori_loop(1, NR, send_z, 0)
        landed = zall.at[it, pl.ds(0, NR - 1)]
        pltpu.make_async_copy(landed, landed, z_sem.at[it, 1]).wait()
        both = jnp.sum(zall[it], axis=0)
        psend[it] = both
        pall[it, c] = both

        def send_p(k, carry):
            to = lax.rem(c + k, NCOL)
            pltpu.make_async_remote_copy(
                psend.at[it], pall.at[it, c], p_sem.at[it, 0], p_sem.at[it, 1],
                device_id=(r, to), device_id_type=MESH,
            ).start()
            return carry

        lax.fori_loop(1, NCOL, send_p, 0)
        landed = pall.at[it, pl.ds(0, NCOL - 1)]
        pltpu.make_async_copy(landed, landed, p_sem.at[it, 1]).wait()
        both = jnp.sum(pall[it], axis=0)
        step = both[0:1, :] / both[1:2, :]
        moved = jnp.clip(lam[...] - step * search[...], -bound[...], bound[...])
        if it < ITERS - 1:
            lam[...] = moved
        else:
            out_ref[...] = moved.astype(BF16)

    sent = asend.at[pl.ds(0, NR - 1)]
    pltpu.make_async_copy(sent, sent, a_sem.at[0]).wait()
    for it in range(ITERS):
        for f in range(4):
            sent = disp.at[it, pl.ds(f * FACE, FACE)]
            pltpu.make_async_copy(sent, sent, face_s.at[it, f]).wait()
        sent = xall.at[it, pl.ds(0, NR - 1), pl.ds(0, NC)]
        pltpu.make_async_copy(sent, sent, x_sem.at[it, 0]).wait()
        sent = parts.at[it, pl.ds(0, NCOL - 1)]
        pltpu.make_async_copy(sent, sent, part_sem.at[it, 0]).wait()
        sent = zall.at[it, pl.ds(0, NR - 1)]
        pltpu.make_async_copy(sent, sent, z_sem.at[it, 0]).wait()
        sent = pall.at[it, pl.ds(0, NCOL - 1)]
        pltpu.make_async_copy(sent, sent, p_sem.at[it, 0]).wait()


def local(*args):
    hbm = pl.BlockSpec(memory_space=pl.ANY)
    smem = pl.BlockSpec(memory_space=pltpu.SMEM)
    dma = pltpu.SemaphoreType.DMA
    v = pltpu.VMEM
    out = pl.pallas_call(
        kernel,
        out_shape=jax.ShapeDtypeStruct((M, R), BF16),
        in_specs=[hbm, hbm, hbm, hbm, hbm, smem, hbm, smem],
        out_specs=pl.BlockSpec(memory_space=pltpu.VMEM),
        scratch_shapes=[
            v((M, R), BF16),
            v((M, M), BF16),
            v((M, M), BF16),
            v((NC, M), F32),
            v((2 * NR * NC, NR * NC), F32),
            v((1, M), jnp.int32),
            v((M, R), F32),
            v((M, R), F32),
            v((ITERS, M, R), F32),
            v((ITERS, M, R), F32),
            v((M, R), F32),
            v((M, R), F32),
            v((M, R), BF16),
            v((M, 128), BF16),
            v((32, M), F32),
            v((NR, 3 * NC, 128), F32),
            v((NR, 3 * NC, 128), F32),
            v((NCOL, 16, 128), F32),
            v((NCOL, 16, 128), F32),
            v((512, 256), BF16),
            v((512, 256), BF16),
            v((ITERS, NC, R), F32),
            v((ITERS, NR, 16, R), F32),
            v((ITERS, NCOL, NC, R), F32),
            v((ITERS, NCOL, NC, R), F32),
            v((ITERS, 2, R), F32),
            v((ITERS, NR, 2, R), F32),
            v((ITERS, 2, R), F32),
            v((ITERS, NCOL, 2, R), F32),
            dma((6,)),
            dma((2,)),
            dma((ITERS, 4)),
            dma((ITERS, 4)),
            dma((ITERS, 2)),
            dma((ITERS, 2)),
            dma((ITERS, 2)),
            dma((ITERS, 2)),
        ],
        compiler_params=pltpu.CompilerParams(
            collective_id=0, has_side_effects=True, vmem_limit_bytes=40 * 1024 * 1024
        ),
        name="feti",
    )(*args)
    return out[None, None]


def solution(mesh):
    cell = P("row", "col", None, None)
    placed = (cell, cell, cell, cell, P("row", "col"), P(), P("row", "col", None), P("row", "col", None))
    return jax.shard_map(local, mesh=mesh, in_specs=placed, out_specs=cell, check_vma=False)
```

```python
import jax
import jax.numpy as jnp
from jax import lax
from jax.experimental import pallas as pl
from jax.experimental.pallas import tpu as pltpu
from jax.sharding import PartitionSpec as P

MESH = pl.DeviceIdType.MESH
F32 = jnp.float32
BF16 = jnp.bfloat16
ITERS = 2
NR = 16
NCOL = 32
M = 1024
FACE = 256
NC = 12
R = 128
LEVELS = 16


def dot(a, b):
    return jnp.dot(a, b, preferred_element_type=F32)


def split(v):
    high = v.astype(BF16)
    low = (v - high.astype(F32)).astype(BF16)
    return high, low


def swing(m):
    return 4 + (1 - 2 * lax.rem(m, 2)) * ((m + 1) // 2)


def each_in_row(r, act):
    z, core = r // 2, lax.rem(r, 2)

    def step(m, carry):
        at = lax.rem(z + swing(m), 8) * 2
        act(at + core)
        act(at + 1 - core)
        return carry

    lax.fori_loop(0, 7, step, 0)
    act(z * 2 + 1 - core)


def each_in_col(c, act):
    x, y = c // 8, lax.rem(c, 8)

    def step(m, carry):
        at = lax.rem(y + swing(m), 8)
        for dx in (2, 1, 3, 0):
            act(lax.rem(x + dx, 4) * 8 + at)
        return carry

    lax.fori_loop(0, 7, step, 0)
    for dx in (2, 1, 3):
        act(lax.rem(x + dx, 4) * 8 + y)


def kernel(
    slip_h, flex_h, schur_h, coup_h, coarse_h, table_h, bidx_h, frows_h, out_ref,
    slip, flex, schur, coup, turned, coarse, bidx, table, frows,
    bound, lam, disp, paired, jump, search, pb_v, ct, c2, cfull, cl, cl_in, g2, fixed, wsend, w_in,
    asend, arecv, aleft, aright, ahi, alo,
    xsend, xall, part, parts, zsend, zall, psend, pall,
    load_sem, a_sem, face_s, face_r, cl_s, cl_r, w_s, w_r, x_sem, part_sem, z_sem, p_sem,
):
    r = lax.axis_index("row")
    c = lax.axis_index("col")

    load_table = pltpu.make_async_copy(table_h, table, load_sem.at[0])
    load_bidx = pltpu.make_async_copy(bidx_h.at[0], bidx, load_sem.at[1])
    load_slip = pltpu.make_async_copy(slip_h.at[0, 0], slip, load_sem.at[2])
    load_flex = pltpu.make_async_copy(flex_h.at[0, 0], flex, load_sem.at[3])
    load_frows = pltpu.make_async_copy(frows_h.at[0], frows, load_sem.at[4])
    load_coup = pltpu.make_async_copy(coup_h, coup, load_sem.at[5])
    load_coarse = pltpu.make_async_copy(coarse_h, turned.at[pl.ds(0, NR * NC)], load_sem.at[6])
    load_schur = pltpu.make_async_copy(schur_h.at[0, 0], schur, load_sem.at[7])
    loads = (
        load_table, load_bidx, load_slip, load_flex, load_frows, load_coup, load_coarse, load_schur
    )
    for copy in loads:
        copy.start()

    xall[:, :, NC:16, :] = jnp.zeros((ITERS, NR, 16 - NC, R), F32)

    barrier = pltpu.get_barrier_semaphore()

    def greet(to):
        pl.semaphore_signal(barrier, inc=1, device_id=to, device_id_type=MESH)

    each_in_col(c, lambda to: greet((r, to)))
    each_in_row(r, lambda to: greet((to, c)))

    load_table.wait()
    load_bidx.wait()
    for q in range(M // 128):
        level = bidx[:, q * 128 : (q + 1) * 128]
        row = jnp.zeros((1, 128), F32)
        for n in range(LEVELS):
            row = jnp.where(level == n, table[n], row)
        bound[q * 128 : (q + 1) * 128, :] = jnp.transpose(jnp.broadcast_to(row, (128, 128)))

    load_slip.wait()
    lam[...] = jnp.clip(slip[...].astype(F32), -bound[...], bound[...])

    up_col, down_col = lax.rem(c + 1, NCOL), lax.rem(c + NCOL - 1, NCOL)
    up_row, down_row = lax.rem(r + 1, NR), lax.rem(r + NR - 1, NR)
    faces = (
        (1, (r, up_col), 0),
        (0, (r, down_col), 1),
        (3, (up_row, c), 2),
        (2, (down_row, c), 3),
    )

    def displace(it, own):
        rows = slice(own * FACE, (own + 1) * FACE)
        disp[it, rows, :] = dot(flex[rows, :], lam[...].astype(BF16))

    def send_face(it, own, to, there):
        pltpu.make_async_remote_copy(
            disp.at[it, pl.ds(own * FACE, FACE)],
            paired.at[it, pl.ds(there * FACE, FACE)],
            face_s.at[it, own],
            face_r.at[it, there],
            device_id=to,
            device_id_type=MESH,
        ).start()

    def find_jump(it):
        for f in range(4):
            rows = slice(f * FACE, (f + 1) * FACE)
            landed = paired.at[it, pl.ds(f * FACE, FACE)]
            pltpu.make_async_copy(landed, landed, face_r.at[it, f]).wait()
            live = lax.broadcasted_iota(jnp.int32, (FACE, R), 0) < frows[0, f]
            gap = disp[it, rows, :] - paired[it, rows, :] - slip[rows, :].astype(F32)
            jump[rows, :] = jnp.where(live, gap, 0.0)

    load_flex.wait()
    for own, to, there in faces:
        displace(0, own)
    pl.semaphore_wait(barrier, NR + NCOL - 2)
    for own, to, there in faces:
        send_face(0, own, to, there)

    load_coarse.wait()
    for i in range(2):
        for j in range(3):
            coarse[j * 128 : (j + 1) * 128, i * 128 : (i + 1) * 128] = jnp.transpose(
                turned[i * 128 : (i + 1) * 128, j * 128 : (j + 1) * 128]
            )
    for a in range(NR):
        lo, hi = a * NC, NR * NC + a * NC
        asend[a, 0:NC, :] = coarse[lo : lo + NC, 0:128]
        asend[a, NC : 2 * NC, :] = coarse[hi : hi + NC, 0:128]
        asend[a, 2 * NC : 3 * NC, 0:64] = coarse[lo : lo + NC, 128:192]
        asend[a, 2 * NC : 3 * NC, 64:128] = coarse[hi : hi + NC, 128:192]

    def send_a(to):
        pltpu.make_async_remote_copy(
            asend.at[to], arecv.at[r], a_sem.at[0], a_sem.at[1], device_id=(to, c), device_id_type=MESH
        ).start()

    each_in_row(r, send_a)
    arecv[r] = asend[r]

    load_coup.wait()
    load_frows.wait()
    for k in range(NC):
        cfull[k : k + 1, :] = coup[k]
    cfull[NC:16, :] = jnp.zeros((4, M), F32)
    coup_hi, coup_lo = split(cfull[...])
    c2[0:16, :] = coup_hi.astype(F32)
    c2[16:32, :] = coup_lo.astype(F32)
    stacked = jnp.concatenate([c2[...], c2[0:16, :], jnp.zeros((80, M), F32)], axis=0)
    for q in range(M // 128):
        ct[q * 128 : (q + 1) * 128, :] = jnp.transpose(stacked[:, q * 128 : (q + 1) * 128]).astype(BF16)
    for f in range(4):
        live = lax.broadcasted_iota(jnp.int32, (16, FACE), 1) < frows[0, f]
        cl[f] = jnp.where(live, cfull[:, f * FACE : (f + 1) * FACE], 0.0)
    for own, to, there in faces:
        pltpu.make_async_remote_copy(
            cl.at[own], cl_in.at[there], cl_s.at[own], cl_r.at[there], device_id=to, device_id_type=MESH
        ).start()
    load_schur.wait()

    def to_bf16_rows(hi, lo):
        return jnp.concatenate([hi.astype(F32), lo.astype(F32)], axis=0).astype(BF16)

    def fold_flex():
        total = jnp.zeros((32, M), F32)
        fix = jnp.zeros((32, R), F32)
        for f in range(4):
            rows = slice(f * FACE, (f + 1) * FACE)
            landed = cl_in.at[f]
            pltpu.make_async_copy(landed, landed, cl_r.at[f]).wait()
            own = to_bf16_rows(*split(cl[f]))
            total = total + dot(own, flex[rows, :])
            fix = fix + dot(own, slip[rows, :])
            across = dot(to_bf16_rows(*split(cl_in[f])), flex[rows, :])
            hi, lo = split(across[0:16] + across[16:32])
            g2[16 + 16 * f : 32 + 16 * f, :] = hi
            g2[96 + 16 * f : 112 + 16 * f, :] = lo
        hi, lo = split(total[0:16] + total[16:32])
        g2[0:16, :] = hi
        g2[80:96, :] = lo
        fixed[...] = fix[0:16] + fix[16:32]

    def unpack_a():
        pltpu.make_async_copy(arecv.at[pl.ds(0, NR - 1)], arecv.at[pl.ds(0, NR - 1)], a_sem.at[1]).wait()
        lane = lax.broadcasted_iota(jnp.int32, (NC, 128), 1)
        zero = jnp.zeros((NC, 128), F32)
        for s in range(NR):
            last = arecv[s, 2 * NC : 3 * NC, :]
            aleft[2 * s, 0:NC, :] = arecv[s, 0:NC, :]
            aleft[2 * s + 1, 0:NC, :] = arecv[s, NC : 2 * NC, :]
            aright[2 * s, 0:NC, :] = jnp.where(lane < 64, last, zero)
            aright[2 * s + 1, 0:NC, :] = jnp.where(lane < 64, zero, last)
        i0 = lax.broadcasted_iota(jnp.int32, (128, 256), 0)
        i1 = lax.broadcasted_iota(jnp.int32, (128, 256), 1)
        index = jnp.where(i1 % 16 < NC, (i1 // 16) * NC + i1 % 16, -1)
        pick_left = (index == i0).astype(F32).astype(BF16)
        pick_right = (index == 128 + i0 % 64).astype(F32).astype(BF16)
        left_hi, left_lo = split(aleft[...].reshape(512, 128))
        right_hi, right_lo = split(aright[...].reshape(512, 128))
        ahi[...] = (dot(left_hi, pick_left) + dot(right_hi, pick_right)).astype(BF16)
        alo[...] = (dot(left_lo, pick_left) + dot(right_lo, pick_right)).astype(BF16)

    aleft[...] = jnp.zeros_like(aleft)
    aright[...] = jnp.zeros_like(aright)

    for it in range(ITERS):
        if it == 0:
            find_jump(it)
            jump_hi, jump_lo = split(jump[...])
            force = dot(c2[...].astype(BF16), jnp.concatenate([jump_hi, jump_lo], axis=1))
            force = force[0:16, 0:R] + (force[0:16, R : 2 * R] + force[16:32, 0:R])
        else:
            adds = dot(g2[...], lam[...].astype(BF16))
            adds = adds[0:80] + adds[80:160]
            for own, to, there in faces:
                wsend[own] = adds[16 + 16 * own : 16 + 16 * own + NC]
                pltpu.make_async_remote_copy(
                    wsend.at[own], w_in.at[there], w_s.at[own], w_r.at[there], device_id=to, device_id_type=MESH
                ).start()
            for own, to, there in faces:
                displace(it, own)
                send_face(it, own, to, there)
            force = adds[0:NC] - fixed[0:NC, :]
            for f in range(4):
                landed = w_in.at[f]
                pltpu.make_async_copy(landed, landed, w_r.at[f]).wait()
                force = force - w_in[f]
        xsend[it] = force[0:NC, :]
        xall[it, r, 0:NC, :] = force[0:NC, :]

        def send_x(to):
            pltpu.make_async_remote_copy(
                xsend.at[it], xall.at[it, r, pl.ds(0, NC)], x_sem.at[it, 0], x_sem.at[it, 1],
                device_id=(to, c), device_id_type=MESH,
            ).start()

        each_in_row(r, send_x)
        if it == 0:
            unpack_a()
        landed = xall.at[it, pl.ds(0, NR - 1), pl.ds(0, NC)]
        pltpu.make_async_copy(landed, landed, x_sem.at[it, 1]).wait()
        x_hi, x_lo = split(xall[it].reshape(256, R))
        both = dot(ahi[...], jnp.concatenate([x_hi, x_lo], axis=1))
        sums = both[:, 0:R] + (both[:, R : 2 * R] + dot(alo[...], x_hi))
        part[it] = sums.reshape(NCOL, 16, R)[:, 0:NC, :]
        parts[it, c] = part[it, c]

        def send_part(to):
            pltpu.make_async_remote_copy(
                part.at[it, to], parts.at[it, c], part_sem.at[it, 0], part_sem.at[it, 1],
                device_id=(r, to), device_id_type=MESH,
            ).start()

        each_in_col(c, send_part)
        if it == 0:
            fold_flex()
        else:
            find_jump(it)
        landed = parts.at[it, pl.ds(0, NCOL - 1)]
        pltpu.make_async_copy(landed, landed, part_sem.at[it, 1]).wait()
        values = jnp.sum(parts[it], axis=0)
        values = jnp.concatenate([values, jnp.zeros((4, R), F32)], axis=0)
        v_hi, v_lo = split(values)
        v_hi, v_lo = v_hi.astype(F32), v_lo.astype(F32)
        stack = jnp.concatenate([v_hi, v_hi, v_lo, jnp.zeros((80, R), F32)], axis=0).astype(BF16)
        p_b = (jump[...] - dot(ct[...], stack)).astype(BF16)
        gain = jnp.zeros((1, R), F32)
        pb_v[...] = p_b
        for f in range(4):
            rows = slice(f * FACE, (f + 1) * FACE)
            s = dot(schur[rows, :], p_b)
            search[rows, :] = s
            gain = gain + jnp.sum(pb_v[rows, :].astype(F32) * s, axis=0, keepdims=True)
        s_b = search[...].astype(BF16)
        curve = jnp.zeros((1, R), F32)
        for f in range(4):
            rows = slice(f * FACE, (f + 1) * FACE)
            curve = curve + jnp.sum(
                search[rows, :].astype(BF16).astype(F32) * dot(flex[rows, :], s_b), axis=0, keepdims=True
            )
        both = jnp.concatenate([gain, curve], axis=0)
        zsend[it] = both
        zall[it, r] = both

        def send_z(to):
            pltpu.make_async_remote_copy(
                zsend.at[it], zall.at[it, r], z_sem.at[it, 0], z_sem.at[it, 1],
                device_id=(to, c), device_id_type=MESH,
            ).start()

        each_in_row(r, send_z)
        landed = zall.at[it, pl.ds(0, NR - 1)]
        pltpu.make_async_copy(landed, landed, z_sem.at[it, 1]).wait()
        both = jnp.sum(zall[it], axis=0)
        psend[it] = both
        pall[it, c] = both

        def send_p(to):
            pltpu.make_async_remote_copy(
                psend.at[it], pall.at[it, c], p_sem.at[it, 0], p_sem.at[it, 1],
                device_id=(r, to), device_id_type=MESH,
            ).start()

        each_in_col(c, send_p)
        landed = pall.at[it, pl.ds(0, NCOL - 1)]
        pltpu.make_async_copy(landed, landed, p_sem.at[it, 1]).wait()
        both = jnp.sum(pall[it], axis=0)
        step = both[0:1, :] / both[1:2, :]
        moved = jnp.clip(lam[...] - step * search[...], -bound[...], bound[...])
        if it < ITERS - 1:
            lam[...] = moved
        else:
            out_ref[...] = moved.astype(BF16)

    sent = asend.at[pl.ds(0, NR - 1)]
    pltpu.make_async_copy(sent, sent, a_sem.at[0]).wait()
    for f in range(4):
        pltpu.make_async_copy(cl.at[f], cl.at[f], cl_s.at[f]).wait()
        pltpu.make_async_copy(wsend.at[f], wsend.at[f], w_s.at[f]).wait()
    for it in range(ITERS):
        for f in range(4):
            sent = disp.at[it, pl.ds(f * FACE, FACE)]
            pltpu.make_async_copy(sent, sent, face_s.at[it, f]).wait()
        sent = xall.at[it, pl.ds(0, NR - 1), pl.ds(0, NC)]
        pltpu.make_async_copy(sent, sent, x_sem.at[it, 0]).wait()
        sent = parts.at[it, pl.ds(0, NCOL - 1)]
        pltpu.make_async_copy(sent, sent, part_sem.at[it, 0]).wait()
        sent = zall.at[it, pl.ds(0, NR - 1)]
        pltpu.make_async_copy(sent, sent, z_sem.at[it, 0]).wait()
        sent = pall.at[it, pl.ds(0, NCOL - 1)]
        pltpu.make_async_copy(sent, sent, p_sem.at[it, 0]).wait()


def local(slip_load, flexibility, schur, corner_coupling, coarse_inverse, bounds_table, bound_index, face_rows):
    hbm = pl.BlockSpec(memory_space=pl.ANY)
    dma = pltpu.SemaphoreType.DMA
    v = pltpu.VMEM
    out = pl.pallas_call(
        kernel,
        out_shape=pltpu.VMEM((M, R), BF16),
        in_specs=[hbm] * 8,
        out_specs=pl.BlockSpec(memory_space=pltpu.VMEM),
        scratch_shapes=[
            v((M, R), BF16),
            v((M, M), BF16),
            v((M, M), BF16),
            v((NC, 1, M), F32),
            v((256, 2 * NR * NC), F32),
            v((2 * NR * NC, 256), F32),
            v((1, M), jnp.int32),
            pltpu.SMEM((LEVELS,), F32),
            pltpu.SMEM((1, 4), jnp.int32),
            v((M, R), F32),
            v((M, R), F32),
            v((ITERS, M, R), F32),
            v((ITERS, M, R), F32),
            v((M, R), F32),
            v((M, R), F32),
            v((M, R), BF16),
            v((M, 128), BF16),
            v((32, M), F32),
            v((16, M), F32),
            v((4, 16, FACE), F32),
            v((4, 16, FACE), F32),
            v((160, M), BF16),
            v((16, R), F32),
            v((4, NC, R), F32),
            v((4, NC, R), F32),
            v((NR, 3 * NC, 128), F32),
            v((NR, 3 * NC, 128), F32),
            v((NCOL, 16, 128), F32),
            v((NCOL, 16, 128), F32),
            v((512, 256), BF16),
            v((512, 256), BF16),
            v((ITERS, NC, R), F32),
            v((ITERS, NR, 16, R), F32),
            v((ITERS, NCOL, NC, R), F32),
            v((ITERS, NCOL, NC, R), F32),
            v((ITERS, 2, R), F32),
            v((ITERS, NR, 2, R), F32),
            v((ITERS, 2, R), F32),
            v((ITERS, NCOL, 2, R), F32),
            dma((8,)),
            dma((2,)),
            dma((ITERS, 4)),
            dma((ITERS, 4)),
            dma((4,)),
            dma((4,)),
            dma((4,)),
            dma((4,)),
            dma((ITERS, 2)),
            dma((ITERS, 2)),
            dma((ITERS, 2)),
            dma((ITERS, 2)),
        ],
        compiler_params=pltpu.CompilerParams(
            collective_id=0, has_side_effects=True, vmem_limit_bytes=56 * 1024 * 1024
        ),
        name="feti",
    )(
        slip_load, flexibility, schur, corner_coupling.reshape(NC, 1, M), coarse_inverse.T,
        bounds_table, bound_index, face_rows,
    )
    return out[None, None]


def solution(mesh):
    cell = P("row", "col", None, None)
    placed = (cell, cell, cell, cell, P("row", "col"), P(), P("row", "col", None), P("row", "col", None))
    return jax.shard_map(local, mesh=mesh, in_specs=placed, out_specs=cell, check_vma=False)
```
